32 devices in a mesh: lon: 8 (over z, y), bin: 4 (over x, core).
Axes of the slice: x: 2, y: 2, z: 4, core: 2. Of those that a mesh axis runs over, the one named last changes fastest.
Arguments:
- adjoint_start: float32 [8, 4, 8, 1024], P('bin', None, None, 'lon'), may hold values from -6 to 6
- base_flux: float32 [8, 8, 1024], P('bin', None, 'lon'), may hold values from 0.1 to 1
- vertical_mixing: float32 [3, 8, 1024], P(None, None, 'lon'), may hold values from 0.05 to 5
- zonal_fraction: float32 [4, 8], replicated, may hold values from 0.02 to 0.98
- meridional_fraction: float32 [4], replicated, may hold values from 0.05 to 0.95
- zonal_hops: int32 [8], replicated, may hold values from -3 to 3, as said below
- cell_shift: int32 [8], replicated, may hold values from 0 to 127, as said below
Outputs:
- adjoint_end: float32 [8, 4, 8, 1024], P('bin', None, None, 'lon')
- emission_gradient: float32 [8, 1024], P(None, 'lon')
The draws below stay inside these ranges and needn't reach their ends.
Inputs may be any that keep to these rules, and one draw needn't show every extreme that they name: For every h from 1 to 3, exactly (3 - h + 1) * 1 rows have zonal_hops >= h and exactly as many have zonal_hops <= -h. `cell_shift`: both extreme values occur.
All inputs are finite; a program needn't handle non-finite values.
Results may differ from the reference program's by a relative error of at most 0.0001.
Values sent between devices are 32-bit elements; how exact they have to be, the bound alone decides.
A program may use at most 64 MiB of HBM per device.

```python
import math
import jax
import jax.numpy as jnp

BINS = 8
LEV = 4
LON_DEV = 128
HMAX = 3
STEPS = 2
NLAT = 8
NLON = 1024


def draw_zonal_hops(key, part):
    half_rows = NLAT // 2
    band_rows = max(1, NLAT // 16)
    polar_index = jnp.arange(half_rows, dtype=jnp.int32)
    magnitude = jnp.maximum(HMAX - polar_index // band_rows, 0).astype(jnp.int32)
    first_key, second_key = jax.random.split(key)
    northern = jax.random.permutation(first_key, magnitude)
    southern = -jax.random.permutation(second_key, magnitude)
    return jnp.concatenate([northern, southern]).astype(jnp.int32)


def draw_cell_shift(key, part):
    rows_index = jnp.arange(NLAT, dtype=jnp.int32)
    drawn = jax.random.randint(jax.random.fold_in(key, 7), (NLAT,), 0, LON_DEV, dtype=jnp.int32)
    drawn = jnp.where(rows_index == NLAT // 2, LON_DEV - 1, drawn)
    drawn = jnp.where(rows_index == NLAT // 2 - 1, 0, drawn)
    return drawn.astype(jnp.int32)


def level_of(own_key, shape, cuts, low, largest):
    loudness = 1.0
    for dim, shards_of in cuts:
        heights = jax.random.uniform(jax.random.fold_in(jax.random.fold_in(own_key, 6), dim), (shards_of,), jnp.float32, low / len(cuts), largest / len(cuts))
        loudness = loudness * jnp.repeat(jnp.exp(heights), shape[dim] // shards_of).reshape((-1,) + (1,) * (len(shape) - 1 - dim))
    return loudness


def gaussian(stream_key, dims, scale, reach, pieces=(), kind=jnp.bfloat16):
    factor_of = level_of(stream_key, dims, pieces, -0.22, 0.18) if pieces else 1.0
    entries = jax.random.normal(stream_key, dims, jnp.float32) * scale * factor_of
    return jnp.minimum(jnp.maximum(entries, -reach), reach).astype(kind)


def setup_inputs(seed: int = 0) -> dict:
    splits = jax.random.split(jax.random.key(seed), 8)
    adjoint_start = gaussian(splits[0], (BINS, LEV, NLAT, NLON), 1.0, 6.0, ((0, 4), (3, 8)), jnp.float32)
    base_flux = jnp.clip(jnp.exp(math.log(1.0) - 2.3025851 * jax.random.uniform(splits[1], (BINS, NLAT, NLON), jnp.float32) ** level_of(splits[1], (BINS, NLAT, NLON), ((0, 4), (2, 8)), -0.2, 0.2)), 0.1, 1.0)
    vertical_mixing = jnp.clip(jnp.exp(math.log(5.0) - 4.6051702 * jax.random.uniform(splits[2], (LEV - 1, NLAT, NLON), jnp.float32) ** level_of(splits[2], (LEV - 1, NLAT, NLON), ((2, 8),), -0.2, 0.2)), 0.05, 5.0)
    zonal_fraction = jnp.clip(jax.random.uniform(splits[3], (LEV, NLAT), jnp.float32, 0.02, 0.98), 0.02, 0.98)
    meridional_fraction = jnp.clip(jax.random.uniform(splits[4], (LEV,), jnp.float32, 0.05, 0.95), 0.05, 0.95)
    zonal_hops = draw_zonal_hops(jax.random.fold_in(splits[7], 71), 0)
    cell_shift = draw_cell_shift(jax.random.fold_in(splits[7], 71), 0)
    return {"adjoint_start": adjoint_start, "base_flux": base_flux, "vertical_mixing": vertical_mixing, "zonal_fraction": zonal_fraction, "meridional_fraction": meridional_fraction, "zonal_hops": zonal_hops, "cell_shift": cell_shift}


right_face = (0.0, -1.0, 7.0, 7.0, -1.0)
slope_face = (1.0, -8.0, 0.0, 8.0, -1.0)
curve_face = (3.0, -18.0, 30.0, -18.0, 3.0)


def flux_weights(courant):
    square = courant * courant
    cubic_part = 0.5 * square * (1.0 - courant * (2.0 / 3.0))
    return [(courant * right_face[offset] - 0.5 * square * slope_face[offset] + cubic_part * curve_face[offset]) / 12.0 for offset in range(5)]


def vertical_solve(adjoint_field, vertical_mixing):
    levels = adjoint_field.shape[1]
    ratios = []
    values = []
    for layer_index in range(levels):
        pivot_value = 1.0
        source_row = adjoint_field[:, layer_index]
        if layer_index < levels - 1:
            pivot_value = pivot_value + vertical_mixing[layer_index]
        if layer_index > 0:
            below = vertical_mixing[layer_index - 1]
            pivot_value = pivot_value + below + below * ratios[-1]
            source_row = source_row + below * values[-1]
        values.append(source_row / pivot_value)
        if layer_index < levels - 1:
            ratios.append(-vertical_mixing[layer_index] / pivot_value)
    solved = [values[levels - 1]]
    for layer_index in range(levels - 2, -1, -1):
        solved.insert(0, values[layer_index] - ratios[layer_index] * solved[0])
    return jnp.stack(solved, axis=1)


def zonal_adjoint(adjoint_field, zonal_fraction):
    weights = flux_weights(zonal_fraction)
    face_flux = 0.0
    for offset in range(5):
        face_flux = face_flux + weights[offset][:, :, None] * jnp.roll(adjoint_field, offset - 2, axis=3)
    return adjoint_field - face_flux + jnp.roll(face_flux, -1, axis=3)


def integer_shift(adjoint_field, zonal_hops, cell_shift):
    total_lon = adjoint_field.shape[3]
    offsets = zonal_hops * LON_DEV + cell_shift
    columns = (jnp.arange(total_lon, dtype=jnp.int32)[None, :] + offsets[:, None]) % total_lon
    return jnp.take_along_axis(adjoint_field, jnp.broadcast_to(columns[None, None], adjoint_field.shape), axis=3)


def meridional_adjoint(adjoint_field, meridional_fraction):
    lat_count = adjoint_field.shape[2]
    weights = flux_weights(meridional_fraction)
    padded = jnp.pad(adjoint_field, ((0, 0), (0, 0), (3, 3), (0, 0)))
    face_flux = 0.0
    for offset in range(5):
        start_row = 3 - (offset - 2)
        face_flux = face_flux + weights[offset][:, None, None] * padded[:, :, start_row:start_row + lat_count + 1]
    return adjoint_field - face_flux[:, :, :lat_count] + face_flux[:, :, 1:]


def reference(adjoint_start, base_flux, vertical_mixing, zonal_fraction, meridional_fraction, zonal_hops, cell_shift):
    adjoint_field = adjoint_start
    gradient_sum = jnp.zeros(base_flux.shape[1:], jnp.float32)
    for step_index in range(STEPS):
        adjoint_field = vertical_solve(adjoint_field, vertical_mixing)
        adjoint_field = zonal_adjoint(adjoint_field, zonal_fraction)
        adjoint_field = integer_shift(adjoint_field, zonal_hops, cell_shift)
        adjoint_field = meridional_adjoint(adjoint_field, meridional_fraction)
        gradient_sum = gradient_sum + jnp.sum(base_flux * adjoint_field[:, 0], axis=0)
    return adjoint_field, gradient_sum
```

```python
import functools

import jax
import jax.numpy as jnp
from jax import lax
from jax.experimental import pallas as pl
from jax.experimental.pallas import tpu as pltpu
from jax.sharding import PartitionSpec as P

HMAX = 3
STEPS = 2
MESH = pl.DeviceIdType.MESH

right_face = (0.0, -1.0, 7.0, 7.0, -1.0)
slope_face = (1.0, -8.0, 0.0, 8.0, -1.0)
curve_face = (3.0, -18.0, 30.0, -18.0, 3.0)


def flux_weights(courant):
    square = courant * courant
    cubic_part = 0.5 * square * (1.0 - courant * (2.0 / 3.0))
    return [
        (
            courant * right_face[offset]
            - 0.5 * square * slope_face[offset]
            + cubic_part * curve_face[offset]
        )
        * (1.0 / 12.0)
        for offset in range(5)
    ]


def taps(courant):
    a = flux_weights(courant)
    return [-a[4], a[4] - a[3], 1.0 + a[3] - a[2], a[2] - a[1], a[1] - a[0], a[0]]


def loop(count, body):
    if count <= 8:
        for i in range(count):
            body(i)
    else:

        @pl.loop(0, count)
        def _(i):
            body(i)


class Plan:
    def __init__(self, rows, unit, ring):
        self.ring = ring
        count = {h: unit for h in range(-HMAX, HMAX + 1)}
        count[0] = rows - 2 * HMAX * unit
        self.count = count
        self.start = {}
        at = 0
        for h in range(-HMAX, HMAX + 1):
            self.start[h] = at
            at += count[h]
        self.offsets = [t for t in range(-HMAX - 2, HMAX + 2) if t % ring]
        self.offsets.sort(key=lambda t: -abs(t))
        self.slot = {t: i for i, t in enumerate(self.offsets)}

    def span(self, t):
        low, high = max(-t - 2, -HMAX), min(-t + 1, HMAX)
        first = self.start[low]
        return first, self.start[high] + self.count[high] - first


def kernel(
    plan,
    nbin,
    adj_ref,
    flux_ref,
    mix_ref,
    zf_ref,
    mf_ref,
    hops_ref,
    cells_ref,
    end_ref,
    grad_ref,
    rank,
    shifts_of,
    natural_c,
    mixed,
    sends,
    recvs,
    wz,
    wm,
    zonal,
    padded,
    result,
    gbuf,
    send_sem,
    recv_sem,
    gsend_sem,
    grecv_sem,
):
    bins, levels, rows, width = adj_ref.shape
    bl = bins * levels
    ring = plan.ring
    lon, mybin = lax.axis_index("lon"), lax.axis_index("bin")

    barrier = pltpu.get_barrier_semaphore()
    shifts = sorted({t % ring for t in plan.offsets})
    for t in shifts:
        pl.semaphore_signal(
            barrier, inc=1, device_id=(lax.rem(lon + ring - t, ring), mybin), device_id_type=MESH
        )
    for o in range(1, nbin):
        pl.semaphore_signal(
            barrier, inc=1, device_id=(lon, lax.rem(mybin + nbin - o, nbin)), device_id_type=MESH
        )

    inverse, ratios, mix = [], [], [mix_ref[l] for l in range(levels - 1)]
    for l in range(levels):
        pivot = 1.0
        if l < levels - 1:
            pivot = pivot + mix[l]
        if l > 0:
            pivot = pivot + mix[l - 1] + mix[l - 1] * ratios[-1]
        inverse.append(1.0 / pivot)
        if l < levels - 1:
            ratios.append(-mix[l] * inverse[l])

    def at(row):
        if isinstance(row, int):
            return pl.ds(row * bl, bl)
        return pl.ds(pl.multiple_of(row * bl, bl), bl)

    def column(index):
        return pl.ds(index, rows, stride=bl)

    def vertical(field):
        for b in range(bins):
            values = []
            for l in range(levels):
                source = field(b, l)
                if l > 0:
                    source = source + mix[l - 1] * values[-1]
                values.append(source * inverse[l])
            solved = values[levels - 1]
            mixed[column(b * levels + levels - 1), :] = solved
            for l in range(levels - 2, -1, -1):
                solved = values[l] - ratios[l] * solved
                mixed[column(b * levels + l), :] = solved

    level_of = lax.rem(lax.broadcasted_iota(jnp.int32, (bl, width), 0), levels)
    lane = lax.broadcasted_iota(jnp.int32, (bl, width), 1)

    def by_level(value):
        out = jnp.full((bl, width), value(0), jnp.float32)
        for l in range(1, levels):
            out = jnp.where(level_of == l, value(l), out)
        return out

    def splat(value):
        return jnp.full((bl, width), value, jnp.int32)

    def fold(one, start):
        if rows <= 8:
            for i in range(rows):
                start = one(i, start)
            return start
        return lax.fori_loop(0, rows, one, start)

    def find_rank(j):
        mine = splat(hops_ref[j])

        def one(i, total):
            ahead = jnp.where(i < j, 1, 0) if rows > 8 else int(i < j)
            return total + jnp.where(splat(hops_ref[i]) < mine + ahead, 1, 0)

        rank[at(j), :] = fold(one, splat(0))

    def ordered(source, p):
        def one(j, value):
            return jnp.where(rank[at(j), :] == p, source(j), value)

        return fold(one, source(0))

    def copies(step):
        found = []
        for t in plan.offsets:
            first, count = plan.span(t)
            part = pl.ds(first * bl, count * bl)
            i = plan.slot[t]
            found.append(
                pltpu.make_async_remote_copy(
                    src_ref=sends.at[step, part],
                    dst_ref=recvs.at[step, i, part],
                    send_sem=send_sem.at[step, i],
                    recv_sem=recv_sem.at[step, i],
                    device_id=(lax.rem(lon + (t % ring), ring), mybin),
                    device_id_type=MESH,
                )
            )
        return found

    def natural(b, l):
        return result[column(b * levels + l), :]

    gradient = None
    for step in range(STEPS):
        vertical(natural if step else (lambda b, l: adj_ref[b, l]))

        def arrange(p):
            sends[step, at(p), :] = ordered(lambda j: mixed[at(j), :], p)

        if step == 0:
            loop(rows, find_rank)
        loop(rows, arrange)

        if step == 0:
            pl.semaphore_wait(barrier, len(shifts) + nbin - 1)
        moving = copies(step)
        for copy in moving:
            copy.start()

        if step == 0:

            def courant(j):
                natural_c[at(j), :] = by_level(lambda l: zf_ref[l, j])

            loop(rows, courant)

            def zonal_weights(p):
                fraction = ordered(lambda j: natural_c[at(j), :], p)
                for s, value in enumerate(taps(fraction)):
                    wz[s, at(p), :] = value
                shifts_of[at(p), :] = ordered(lambda j: splat(cells_ref[j]), p)

            loop(rows, zonal_weights)
            for s, value in enumerate(taps(by_level(lambda l: mf_ref[l]))):
                wm[s] = value
            nothing = jnp.zeros((bl, width), jnp.float32)
            for row in (0, 1, rows + 2, rows + 3, rows + 4):
                padded[at(row), :] = nothing
        else:
            gradient = sum(flux_ref[b] * natural(b, 0) for b in range(bins))

        for copy in moving:
            copy.wait_recv()

        for h in range(-HMAX, HMAX + 1):

            def shift(i):
                p = plan.start[h] + i

                def tile(k):
                    t = -h - k
                    if t % ring == 0:
                        return sends[step, at(p), :]
                    return recvs[step, plan.slot[t], at(p), :]

                cells = shifts_of[at(p), :]
                short = cells < 2
                first = cells - 2 + jnp.where(short, width, 0)
                t0, t1, t2, t3 = tile(-1), tile(0), tile(1), tile(2)
                ra = jnp.where(short, t0, t1)
                rb = jnp.where(short, t1, t2)
                rc = jnp.where(short, t2, t3)
                for bit in range((width - 1).bit_length()):
                    chosen = (first & (1 << bit)) != 0
                    turn = width - (1 << bit)
                    ra = jnp.where(chosen, pltpu.roll(ra, turn, 1), ra)
                    rb = jnp.where(chosen, pltpu.roll(rb, turn, 1), rb)
                    rc = jnp.where(chosen, pltpu.roll(rc, turn, 1), rc)
                inside = lane < width - first
                w0 = jnp.where(inside, ra, rb)
                w1 = jnp.where(inside, rb, rc)
                out = wz[0, at(p), :] * w0
                for s in range(1, 6):
                    moved = pltpu.roll(jnp.where(lane < s, w1, w0), width - s, 1)
                    out = out + wz[s, at(p), :] * moved
                zonal[at(p), :] = out

            loop(plan.count[h], shift)

        def back(j):
            place = rank[at(j), :]

            def one(p, value):
                return jnp.where(place == p, zonal[at(p), :], value)

            padded[at(j + 2), :] = fold(one, zonal[at(0), :])

        loop(rows, back)

        def meridional(j):
            out = wm[0] * padded[at(j), :]
            for s in range(1, 6):
                out = out + wm[s] * padded[at(j + s), :]
            result[at(j), :] = out

        loop(rows, meridional)

    gradient = gradient + sum(flux_ref[b] * natural(b, 0) for b in range(bins))
    gbuf[mybin] = gradient
    reducing = []
    for o in range(1, nbin):
        copy = pltpu.make_async_remote_copy(
            src_ref=gbuf.at[mybin],
            dst_ref=gbuf.at[mybin],
            send_sem=gsend_sem.at[o - 1],
            recv_sem=grecv_sem.at[o - 1],
            device_id=(lon, lax.rem(mybin + o, nbin)),
            device_id_type=MESH,
        )
        copy.start()
        reducing.append(copy)
    for b in range(bins):
        for l in range(levels):
            end_ref[b, l] = natural(b, l)
    for step in range(STEPS):
        for copy in copies(step):
            copy.wait_send()
    for o in range(1, nbin):
        source = lax.rem(mybin + nbin - o, nbin)
        pltpu.make_async_remote_copy(
            src_ref=gbuf.at[source],
            dst_ref=gbuf.at[source],
            send_sem=gsend_sem.at[o - 1],
            recv_sem=grecv_sem.at[o - 1],
            device_id=(lon, lax.rem(mybin + o, nbin)),
            device_id_type=MESH,
        ).wait_recv()
    total = gbuf[0]
    for o in range(1, nbin):
        total = total + gbuf[o]
    grad_ref[...] = total
    for copy in reducing:
        copy.wait_send()


def per_device(
    ring,
    nbin,
    adjoint_start,
    base_flux,
    vertical_mixing,
    zonal_fraction,
    meridional_fraction,
    zonal_hops,
    cell_shift,
):
    bins, levels, rows, width = adjoint_start.shape
    bl = bins * levels
    plan = Plan(rows, max(1, rows // 16), ring)
    slots = len(plan.offsets)
    vmem = pl.BlockSpec(memory_space=pltpu.VMEM)
    smem = pl.BlockSpec(memory_space=pltpu.SMEM)
    f32 = jnp.float32
    tile = rows * bl
    return pl.pallas_call(
        functools.partial(kernel, plan, nbin),
        out_shape=(
            jax.ShapeDtypeStruct(adjoint_start.shape, f32),
            jax.ShapeDtypeStruct((rows, width), f32),
        ),
        in_specs=[vmem] * 3 + [smem] * 4,
        out_specs=(vmem, vmem),
        scratch_shapes=[
            pltpu.VMEM((tile, width), jnp.int32),
            pltpu.VMEM((tile, width), jnp.int32),
            pltpu.VMEM((tile, width), f32),
            pltpu.VMEM((tile, width), f32),
            pltpu.VMEM((STEPS, tile, width), f32),
            pltpu.VMEM((STEPS, slots, tile, width), f32),
            pltpu.VMEM((6, tile, width), f32),
            pltpu.VMEM((6, bl, width), f32),
            pltpu.VMEM((tile, width), f32),
            pltpu.VMEM(((rows + 5) * bl, width), f32),
            pltpu.VMEM((tile, width), f32),
            pltpu.VMEM((nbin, rows, width), f32),
            pltpu.SemaphoreType.DMA((STEPS, slots)),
            pltpu.SemaphoreType.DMA((STEPS, slots)),
            pltpu.SemaphoreType.DMA((nbin - 1,)),
            pltpu.SemaphoreType.DMA((nbin - 1,)),
        ],
        compiler_params=pltpu.CompilerParams(
            collective_id=0, has_side_effects=True, vmem_limit_bytes=32 * 1024 * 1024
        ),
    )(
        adjoint_start,
        base_flux,
        vertical_mixing,
        zonal_fraction,
        meridional_fraction,
        zonal_hops,
        cell_shift,
    )


def solution(mesh):
    return jax.shard_map(
        functools.partial(per_device, mesh.shape["lon"], mesh.shape["bin"]),
        mesh=mesh,
        in_specs=(
            P("bin", None, None, "lon"),
            P("bin", None, "lon"),
            P(None, None, "lon"),
            P(),
            P(),
            P(),
            P(),
        ),
        out_specs=(P("bin", None, None, "lon"), P(None, "lon")),
        check_vma=False,
    )
```

```python
import functools

import jax
import jax.numpy as jnp
from jax import lax
from jax.experimental import pallas as pl
from jax.experimental.pallas import tpu as pltpu
from jax.sharding import PartitionSpec as P

HMAX = 3
STEPS = 2
MESH = pl.DeviceIdType.MESH

right_face = (0.0, -1.0, 7.0, 7.0, -1.0)
slope_face = (1.0, -8.0, 0.0, 8.0, -1.0)
curve_face = (3.0, -18.0, 30.0, -18.0, 3.0)


def flux_weights(courant):
    square = courant * courant
    cubic_part = 0.5 * square * (1.0 - courant * (2.0 / 3.0))
    return [
        (
            courant * right_face[offset]
            - 0.5 * square * slope_face[offset]
            + cubic_part * curve_face[offset]
        )
        * (1.0 / 12.0)
        for offset in range(5)
    ]


def taps(courant):
    a = flux_weights(courant)
    return [-a[4], a[4] - a[3], 1.0 + a[3] - a[2], a[2] - a[1], a[1] - a[0], a[0]]


def loop(count, body):
    if count <= 8:
        for i in range(count):
            body(i)
    else:

        @pl.loop(0, count)
        def _(i):
            body(i)


class Plan:
    def __init__(self, rows, unit, ring):
        self.ring = ring
        count = {h: unit for h in range(-HMAX, HMAX + 1)}
        count[0] = rows - 2 * HMAX * unit
        self.count = count
        self.start = {}
        at = 0
        for h in range(-HMAX, HMAX + 1):
            self.start[h] = at
            at += count[h]
        self.offsets = [t for t in range(-HMAX - 2, HMAX + 2) if t % ring]
        self.offsets.sort(key=lambda t: -abs(t))
        self.slot = {t: i for i, t in enumerate(self.offsets)}

    def span(self, t):
        low, high = max(-t - 2, -HMAX), min(-t + 1, HMAX)
        first = self.start[low]
        return first, self.start[high] + self.count[high] - first


def kernel(
    plan,
    nbin,
    adj_hbm,
    flux_hbm,
    mix_hbm,
    zf_hbm,
    mf_hbm,
    hops_hbm,
    cells_hbm,
    end_ref,
    grad_ref,
    adj_ref,
    mix_ref,
    flux_ref,
    zf_ref,
    mf_ref,
    hops_ref,
    cells_ref,
    load_sem,
    rank,
    shifts_of,
    natural_c,
    mixed,
    sends,
    recvs,
    wz,
    wm,
    zonal,
    padded,
    result,
    gbuf,
    send_sem,
    recv_sem,
    gsend_sem,
    grecv_sem,
):
    bins, levels, rows, width = adj_ref.shape
    bl = bins * levels
    ring = plan.ring
    lon, mybin = lax.axis_index("lon"), lax.axis_index("bin")

    pairs = (
        (mix_hbm, mix_ref),
        (adj_hbm, adj_ref),
        (hops_hbm, hops_ref),
        (zf_hbm, zf_ref),
        (cells_hbm, cells_ref),
        (mf_hbm, mf_ref),
        (flux_hbm, flux_ref),
    )
    loads = [
        pltpu.make_async_copy(source, target, load_sem.at[i])
        for i, (source, target) in enumerate(pairs)
    ]
    for load in loads:
        load.start()

    barrier = pltpu.get_barrier_semaphore()
    shifts = sorted({t % ring for t in plan.offsets})
    for t in shifts:
        pl.semaphore_signal(
            barrier, inc=1, device_id=(lax.rem(lon + ring - t, ring), mybin), device_id_type=MESH
        )
    for o in range(1, nbin):
        pl.semaphore_signal(
            barrier, inc=1, device_id=(lon, lax.rem(mybin + nbin - o, nbin)), device_id_type=MESH
        )

    for load in loads[:3]:
        load.wait()

    inverse, ratios, mix = [], [], [mix_ref[l] for l in range(levels - 1)]
    for l in range(levels):
        pivot = 1.0
        if l < levels - 1:
            pivot = pivot + mix[l]
        if l > 0:
            pivot = pivot + mix[l - 1] + mix[l - 1] * ratios[-1]
        inverse.append(1.0 / pivot)
        if l < levels - 1:
            ratios.append(-mix[l] * inverse[l])

    def at(row):
        if isinstance(row, int):
            return pl.ds(row * bl, bl)
        return pl.ds(pl.multiple_of(row * bl, bl), bl)

    def column(index):
        return pl.ds(index, rows, stride=bl)

    def vertical(field):
        for b in range(bins):
            values = []
            for l in range(levels):
                source = field(b, l)
                if l > 0:
                    source = source + mix[l - 1] * values[-1]
                values.append(source * inverse[l])
            solved = values[levels - 1]
            mixed[column(b * levels + levels - 1), :] = solved
            for l in range(levels - 2, -1, -1):
                solved = values[l] - ratios[l] * solved
                mixed[column(b * levels + l), :] = solved

    level_of = lax.rem(lax.broadcasted_iota(jnp.int32, (bl, width), 0), levels)
    lane = lax.broadcasted_iota(jnp.int32, (bl, width), 1)

    def by_level(value):
        out = jnp.full((bl, width), value(0), jnp.float32)
        for l in range(1, levels):
            out = jnp.where(level_of == l, value(l), out)
        return out

    def splat(value):
        return jnp.full((bl, width), value, jnp.int32)

    def fold(one, start):
        if rows <= 8:
            for i in range(rows):
                start = one(i, start)
            return start
        return lax.fori_loop(0, rows, one, start)

    def find_rank(j):
        mine = splat(hops_ref[j])

        def one(i, total):
            ahead = jnp.where(i < j, 1, 0) if rows > 8 else int(i < j)
            return total + jnp.where(splat(hops_ref[i]) < mine + ahead, 1, 0)

        rank[at(j), :] = fold(one, splat(0))

    def ordered(source, p):
        def one(j, value):
            return jnp.where(rank[at(j), :] == p, source(j), value)

        return fold(one, source(0))

    def copies(step):
        found = []
        for t in plan.offsets:
            first, count = plan.span(t)
            part = pl.ds(first * bl, count * bl)
            i = plan.slot[t]
            found.append(
                pltpu.make_async_remote_copy(
                    src_ref=sends.at[step, part],
                    dst_ref=recvs.at[step, i, part],
                    send_sem=send_sem.at[step, i],
                    recv_sem=recv_sem.at[step, i],
                    device_id=(lax.rem(lon + (t % ring), ring), mybin),
                    device_id_type=MESH,
                )
            )
        return found

    def natural(b, l):
        return result[column(b * levels + l), :]

    gradient = None
    for step in range(STEPS):
        vertical(natural if step else (lambda b, l: adj_ref[b, l]))

        def arrange(p):
            sends[step, at(p), :] = ordered(lambda j: mixed[at(j), :], p)

        if step == 0:
            loop(rows, find_rank)
        loop(rows, arrange)

        if step == 0:
            pl.semaphore_wait(barrier, len(shifts) + nbin - 1)
        moving = copies(step)
        for copy in moving:
            copy.start()

        if step == 0:
            for load in loads[3:]:
                load.wait()

            def courant(j):
                natural_c[at(j), :] = by_level(lambda l: zf_ref[l, j])

            loop(rows, courant)

            def zonal_weights(p):
                fraction = ordered(lambda j: natural_c[at(j), :], p)
                for s, value in enumerate(taps(fraction)):
                    wz[s, at(p), :] = value
                shifts_of[at(p), :] = ordered(lambda j: splat(cells_ref[j]), p)

            loop(rows, zonal_weights)
            for s, value in enumerate(taps(by_level(lambda l: mf_ref[l]))):
                wm[s] = value
            nothing = jnp.zeros((bl, width), jnp.float32)
            for row in (0, 1, rows + 2, rows + 3, rows + 4):
                padded[at(row), :] = nothing
        else:
            gradient = sum(flux_ref[b] * natural(b, 0) for b in range(bins))

        for copy in moving:
            copy.wait_recv()

        for h in range(-HMAX, HMAX + 1):

            def shift(i):
                p = plan.start[h] + i

                def tile(k):
                    t = -h - k
                    if t % ring == 0:
                        return sends[step, at(p), :]
                    return recvs[step, plan.slot[t], at(p), :]

                cells = shifts_of[at(p), :]
                short = cells < 2
                first = cells - 2 + jnp.where(short, width, 0)
                t0, t1, t2, t3 = tile(-1), tile(0), tile(1), tile(2)
                ra = jnp.where(short, t0, t1)
                rb = jnp.where(short, t1, t2)
                rc = jnp.where(short, t2, t3)
                for bit in range((width - 1).bit_length()):
                    chosen = (first & (1 << bit)) != 0
                    turn = width - (1 << bit)
                    ra = jnp.where(chosen, pltpu.roll(ra, turn, 1), ra)
                    rb = jnp.where(chosen, pltpu.roll(rb, turn, 1), rb)
                    rc = jnp.where(chosen, pltpu.roll(rc, turn, 1), rc)
                inside = lane < width - first
                w0 = jnp.where(inside, ra, rb)
                w1 = jnp.where(inside, rb, rc)
                out = wz[0, at(p), :] * w0
                for s in range(1, 6):
                    moved = pltpu.roll(jnp.where(lane < s, w1, w0), width - s, 1)
                    out = out + wz[s, at(p), :] * moved
                zonal[at(p), :] = out

            loop(plan.count[h], shift)

        def back(j):
            place = rank[at(j), :]

            def one(p, value):
                return jnp.where(place == p, zonal[at(p), :], value)

            padded[at(j + 2), :] = fold(one, zonal[at(0), :])

        loop(rows, back)

        def meridional(j):
            out = wm[0] * padded[at(j), :]
            for s in range(1, 6):
                out = out + wm[s] * padded[at(j + s), :]
            result[at(j), :] = out

        loop(rows, meridional)

    gradient = gradient + sum(flux_ref[b] * natural(b, 0) for b in range(bins))
    gbuf[mybin] = gradient
    reducing = []
    for o in range(1, nbin):
        copy = pltpu.make_async_remote_copy(
            src_ref=gbuf.at[mybin],
            dst_ref=gbuf.at[mybin],
            send_sem=gsend_sem.at[o - 1],
            recv_sem=grecv_sem.at[o - 1],
            device_id=(lon, lax.rem(mybin + o, nbin)),
            device_id_type=MESH,
        )
        copy.start()
        reducing.append(copy)
    for b in range(bins):
        for l in range(levels):
            end_ref[b, l] = natural(b, l)
    for step in range(STEPS):
        for copy in copies(step):
            copy.wait_send()
    for o in range(1, nbin):
        source = lax.rem(mybin + nbin - o, nbin)
        pltpu.make_async_remote_copy(
            src_ref=gbuf.at[source],
            dst_ref=gbuf.at[source],
            send_sem=gsend_sem.at[o - 1],
            recv_sem=grecv_sem.at[o - 1],
            device_id=(lon, lax.rem(mybin + o, nbin)),
            device_id_type=MESH,
        ).wait_recv()
    total = gbuf[0]
    for o in range(1, nbin):
        total = total + gbuf[o]
    grad_ref[...] = total
    for copy in reducing:
        copy.wait_send()


def per_device(
    ring,
    nbin,
    adjoint_start,
    base_flux,
    vertical_mixing,
    zonal_fraction,
    meridional_fraction,
    zonal_hops,
    cell_shift,
):
    bins, levels, rows, width = adjoint_start.shape
    bl = bins * levels
    plan = Plan(rows, max(1, rows // 16), ring)
    slots = len(plan.offsets)
    vmem = pl.BlockSpec(memory_space=pltpu.VMEM)
    f32 = jnp.float32
    tile = rows * bl
    return pl.pallas_call(
        functools.partial(kernel, plan, nbin),
        out_shape=(
            jax.ShapeDtypeStruct(adjoint_start.shape, f32),
            jax.ShapeDtypeStruct((rows, width), f32),
        ),
        in_specs=[pl.BlockSpec(memory_space=pltpu.HBM)] * 7,
        out_specs=(vmem, vmem),
        scratch_shapes=[
            pltpu.VMEM(adjoint_start.shape, f32),
            pltpu.VMEM(vertical_mixing.shape, f32),
            pltpu.VMEM(base_flux.shape, f32),
            pltpu.SMEM(zonal_fraction.shape, f32),
            pltpu.SMEM(meridional_fraction.shape, f32),
            pltpu.SMEM(zonal_hops.shape, jnp.int32),
            pltpu.SMEM(cell_shift.shape, jnp.int32),
            pltpu.SemaphoreType.DMA((7,)),
            pltpu.VMEM((tile, width), jnp.int32),
            pltpu.VMEM((tile, width), jnp.int32),
            pltpu.VMEM((tile, width), f32),
            pltpu.VMEM((tile, width), f32),
            pltpu.VMEM((STEPS, tile, width), f32),
            pltpu.VMEM((STEPS, slots, tile, width), f32),
            pltpu.VMEM((6, tile, width), f32),
            pltpu.VMEM((6, bl, width), f32),
            pltpu.VMEM((tile, width), f32),
            pltpu.VMEM(((rows + 5) * bl, width), f32),
            pltpu.VMEM((tile, width), f32),
            pltpu.VMEM((nbin, rows, width), f32),
            pltpu.SemaphoreType.DMA((STEPS, slots)),
            pltpu.SemaphoreType.DMA((STEPS, slots)),
            pltpu.SemaphoreType.DMA((nbin - 1,)),
            pltpu.SemaphoreType.DMA((nbin - 1,)),
        ],
        compiler_params=pltpu.CompilerParams(
            collective_id=0, has_side_effects=True, vmem_limit_bytes=32 * 1024 * 1024
        ),
    )(
        adjoint_start,
        base_flux,
        vertical_mixing,
        zonal_fraction,
        meridional_fraction,
        zonal_hops,
        cell_shift,
    )


def solution(mesh):
    return jax.shard_map(
        functools.partial(per_device, mesh.shape["lon"], mesh.shape["bin"]),
        mesh=mesh,
        in_specs=(
            P("bin", None, None, "lon"),
            P("bin", None, "lon"),
            P(None, None, "lon"),
            P(),
            P(),
            P(),
            P(),
        ),
        out_specs=(P("bin", None, None, "lon"), P(None, "lon")),
        check_vma=False,
    )
```

```python
import functools

import jax
import jax.numpy as jnp
from jax import lax
from jax.experimental import pallas as pl
from jax.experimental.pallas import tpu as pltpu
from jax.sharding import PartitionSpec as P

HMAX = 3
STEPS = 2
MESH = pl.DeviceIdType.MESH

right_face = (0.0, -1.0, 7.0, 7.0, -1.0)
slope_face = (1.0, -8.0, 0.0, 8.0, -1.0)
curve_face = (3.0, -18.0, 30.0, -18.0, 3.0)


def flux_weights(courant):
    square = courant * courant
    cubic_part = 0.5 * square * (1.0 - courant * (2.0 / 3.0))
    return [
        (
            courant * right_face[offset]
            - 0.5 * square * slope_face[offset]
            + cubic_part * curve_face[offset]
        )
        * (1.0 / 12.0)
        for offset in range(5)
    ]


def taps(courant):
    a = flux_weights(courant)
    return [-a[4], a[4] - a[3], 1.0 + a[3] - a[2], a[2] - a[1], a[1] - a[0], a[0]]


def loop(count, body):
    if count <= 8:
        for i in range(count):
            body(i)
    else:

        @pl.loop(0, count)
        def _(i):
            body(i)


class Plan:
    def __init__(self, rows, unit, ring):
        self.ring = ring
        count = {h: unit for h in range(-HMAX, HMAX + 1)}
        count[0] = rows - 2 * HMAX * unit
        self.count = count
        self.start = {}
        at = 0
        for h in range(-HMAX, HMAX + 1):
            self.start[h] = at
            at += count[h]
        self.rows = rows
        self.extra = 2 * unit
        groups = {}
        for t in range(-HMAX - 2, HMAX + 2):
            if t % ring:
                groups.setdefault(t % ring, []).append(t)
        self.shifts = sorted(groups, key=lambda r: -min(r, ring - r))
        self.slot = {r: i for i, r in enumerate(self.shifts)}
        self.part, self.lift = {}, {}
        for r, both in groups.items():
            first, count = self.span(both[0])
            self.lift[both[0]] = 0
            if len(both) == 2:
                self.lift[both[1]] = rows
                count = rows - first + self.span(both[1])[1]
            self.part[r] = first, count

    def span(self, t):
        low, high = max(-t - 2, -HMAX), min(-t + 1, HMAX)
        first = self.start[low]
        return first, self.start[high] + self.count[high] - first


def kernel(
    plan,
    nbin,
    adj_hbm,
    flux_hbm,
    mix_hbm,
    zf_hbm,
    mf_hbm,
    hops_hbm,
    cells_hbm,
    end_ref,
    grad_ref,
    adj_ref,
    mix_ref,
    flux_ref,
    zf_ref,
    mf_ref,
    hops_ref,
    cells_ref,
    load_sem,
    rank,
    shifts_of,
    natural_c,
    mixed,
    sends,
    recvs,
    wz,
    wm,
    zonal,
    padded,
    result,
    gbuf,
    send_sem,
    recv_sem,
    gsend_sem,
    grecv_sem,
):
    bins, levels, rows, width = adj_ref.shape
    bl = bins * levels
    ring = plan.ring
    lon, mybin = lax.axis_index("lon"), lax.axis_index("bin")

    pairs = (
        (mix_hbm, mix_ref),
        (adj_hbm, adj_ref),
        (hops_hbm, hops_ref),
        (zf_hbm, zf_ref),
        (cells_hbm, cells_ref),
        (mf_hbm, mf_ref),
        (flux_hbm, flux_ref),
    )
    loads = [
        pltpu.make_async_copy(source, target, load_sem.at[i])
        for i, (source, target) in enumerate(pairs)
    ]
    for load in loads:
        load.start()

    barrier = pltpu.get_barrier_semaphore()
    shifts = plan.shifts
    for t in shifts:
        pl.semaphore_signal(
            barrier, inc=1, device_id=(lax.rem(lon + ring - t, ring), mybin), device_id_type=MESH
        )
    for o in range(1, nbin):
        pl.semaphore_signal(
            barrier, inc=1, device_id=(lon, lax.rem(mybin + nbin - o, nbin)), device_id_type=MESH
        )

    for load in loads[:3]:
        load.wait()

    inverse, ratios, mix = [], [], [mix_ref[l] for l in range(levels - 1)]
    for l in range(levels):
        pivot = 1.0
        if l < levels - 1:
            pivot = pivot + mix[l]
        if l > 0:
            pivot = pivot + mix[l - 1] + mix[l - 1] * ratios[-1]
        inverse.append(1.0 / pivot)
        if l < levels - 1:
            ratios.append(-mix[l] * inverse[l])

    def at(row):
        if isinstance(row, int):
            return pl.ds(row * bl, bl)
        return pl.ds(pl.multiple_of(row * bl, bl), bl)

    def column(index):
        return pl.ds(index, rows, stride=bl)

    def vertical(field):
        for b in range(bins):
            values = []
            for l in range(levels):
                source = field(b, l)
                if l > 0:
                    source = source + mix[l - 1] * values[-1]
                values.append(source * inverse[l])
            solved = values[levels - 1]
            mixed[column(b * levels + levels - 1), :] = solved
            for l in range(levels - 2, -1, -1):
                solved = values[l] - ratios[l] * solved
                mixed[column(b * levels + l), :] = solved

    level_of = lax.rem(lax.broadcasted_iota(jnp.int32, (bl, width), 0), levels)
    lane = lax.broadcasted_iota(jnp.int32, (bl, width), 1)

    def by_level(value):
        out = jnp.full((bl, width), value(0), jnp.float32)
        for l in range(1, levels):
            out = jnp.where(level_of == l, value(l), out)
        return out

    def splat(value):
        return jnp.full((bl, width), value, jnp.int32)

    def fold(one, start):
        if rows <= 8:
            for i in range(rows):
                start = one(i, start)
            return start
        return lax.fori_loop(0, rows, one, start)

    def find_rank(j):
        mine = splat(hops_ref[j])

        def one(i, total):
            ahead = jnp.where(i < j, 1, 0) if rows > 8 else int(i < j)
            return total + jnp.where(splat(hops_ref[i]) < mine + ahead, 1, 0)

        rank[at(j), :] = fold(one, splat(0))

    def ordered(source, p):
        def one(j, value):
            return jnp.where(rank[at(j), :] == p, source(j), value)

        return fold(one, source(0))

    def copies(step):
        found = []
        for r in plan.shifts:
            first, count = plan.part[r]
            part = pl.ds(first * bl, count * bl)
            i = plan.slot[r]
            found.append(
                pltpu.make_async_remote_copy(
                    src_ref=sends.at[step, part],
                    dst_ref=recvs.at[step, i, part],
                    send_sem=send_sem.at[step, i],
                    recv_sem=recv_sem.at[step, i],
                    device_id=(lax.rem(lon + r, ring), mybin),
                    device_id_type=MESH,
                )
            )
        return found

    def natural(b, l):
        return result[column(b * levels + l), :]

    gradient = None
    for step in range(STEPS):
        vertical(natural if step else (lambda b, l: adj_ref[b, l]))

        def arrange(p):
            sends[step, at(p), :] = ordered(lambda j: mixed[at(j), :], p)

        if step == 0:
            loop(rows, find_rank)
        loop(rows, arrange)
        for p in range(plan.extra):
            sends[step, at(rows + p), :] = sends[step, at(p), :]

        if step == 0:
            pl.semaphore_wait(barrier, len(shifts) + nbin - 1)
        moving = copies(step)
        for copy in moving:
            copy.start()

        if step == 0:
            for load in loads[3:]:
                load.wait()

            def courant(j):
                natural_c[at(j), :] = by_level(lambda l: zf_ref[l, j])

            loop(rows, courant)

            def zonal_weights(p):
                fraction = ordered(lambda j: natural_c[at(j), :], p)
                for s, value in enumerate(taps(fraction)):
                    wz[s, at(p), :] = value
                shifts_of[at(p), :] = ordered(lambda j: splat(cells_ref[j]), p)

            loop(rows, zonal_weights)
            for s, value in enumerate(taps(by_level(lambda l: mf_ref[l]))):
                wm[s] = value
            nothing = jnp.zeros((bl, width), jnp.float32)
            for row in (0, 1, rows + 2, rows + 3, rows + 4):
                padded[at(row), :] = nothing
        else:
            gradient = sum(flux_ref[b] * natural(b, 0) for b in range(bins))

        arrived = set()
        for h in sorted(range(-HMAX, HMAX + 1), key=abs):
            for r in sorted({(-h - k) % ring for k in range(-1, 3)} - arrived - {0}):
                moving[plan.slot[r]].wait_recv()
                arrived.add(r)

            def shift(i):
                p = plan.start[h] + i

                def tile(k):
                    t = -h - k
                    if t % ring == 0:
                        return sends[step, at(p), :]
                    return recvs[step, plan.slot[t % ring], at(p + plan.lift[t]), :]

                cells = shifts_of[at(p), :]
                short = cells < 2
                first = cells - 2 + jnp.where(short, width, 0)
                t0, t1, t2, t3 = tile(-1), tile(0), tile(1), tile(2)
                ra = jnp.where(short, t0, t1)
                rb = jnp.where(short, t1, t2)
                rc = jnp.where(short, t2, t3)
                source = jnp.where(lane < width - first, lane + first, lane + first - width)
                ra = jnp.take_along_axis(ra, source, axis=1, mode="promise_in_bounds")
                rb = jnp.take_along_axis(rb, source, axis=1, mode="promise_in_bounds")
                rc = jnp.take_along_axis(rc, source, axis=1, mode="promise_in_bounds")
                inside = lane < width - first
                w0 = jnp.where(inside, ra, rb)
                w1 = jnp.where(inside, rb, rc)
                out = wz[0, at(p), :] * w0
                for s in range(1, 6):
                    moved = pltpu.roll(jnp.where(lane < s, w1, w0), width - s, 1)
                    out = out + wz[s, at(p), :] * moved
                zonal[at(p), :] = out

            loop(plan.count[h], shift)

        def back(j):
            place = rank[at(j), :]

            def one(p, value):
                return jnp.where(place == p, zonal[at(p), :], value)

            padded[at(j + 2), :] = fold(one, zonal[at(0), :])

        loop(rows, back)

        def meridional(j):
            out = wm[0] * padded[at(j), :]
            for s in range(1, 6):
                out = out + wm[s] * padded[at(j + s), :]
            result[at(j), :] = out

        loop(rows, meridional)

    gradient = gradient + sum(flux_ref[b] * natural(b, 0) for b in range(bins))
    gbuf[mybin] = gradient
    reducing = []
    for o in range(1, nbin):
        copy = pltpu.make_async_remote_copy(
            src_ref=gbuf.at[mybin],
            dst_ref=gbuf.at[mybin],
            send_sem=gsend_sem.at[o - 1],
            recv_sem=grecv_sem.at[o - 1],
            device_id=(lon, lax.rem(mybin + o, nbin)),
            device_id_type=MESH,
        )
        copy.start()
        reducing.append(copy)
    for b in range(bins):
        for l in range(levels):
            end_ref[b, l] = natural(b, l)
    for step in range(STEPS):
        for copy in copies(step):
            copy.wait_send()
    for o in range(1, nbin):
        source = lax.rem(mybin + nbin - o, nbin)
        pltpu.make_async_remote_copy(
            src_ref=gbuf.at[source],
            dst_ref=gbuf.at[source],
            send_sem=gsend_sem.at[o - 1],
            recv_sem=grecv_sem.at[o - 1],
            device_id=(lon, lax.rem(mybin + o, nbin)),
            device_id_type=MESH,
        ).wait_recv()
    total = gbuf[0]
    for o in range(1, nbin):
        total = total + gbuf[o]
    grad_ref[...] = total
    for copy in reducing:
        copy.wait_send()


def per_device(
    ring,
    nbin,
    adjoint_start,
    base_flux,
    vertical_mixing,
    zonal_fraction,
    meridional_fraction,
    zonal_hops,
    cell_shift,
):
    bins, levels, rows, width = adjoint_start.shape
    bl = bins * levels
    plan = Plan(rows, max(1, rows // 16), ring)
    slots = len(plan.shifts)
    sent = (rows + plan.extra) * bl
    vmem = pl.BlockSpec(memory_space=pltpu.VMEM)
    f32 = jnp.float32
    tile = rows * bl
    return pl.pallas_call(
        functools.partial(kernel, plan, nbin),
        out_shape=(
            jax.ShapeDtypeStruct(adjoint_start.shape, f32),
            jax.ShapeDtypeStruct((rows, width), f32),
        ),
        in_specs=[pl.BlockSpec(memory_space=pltpu.HBM)] * 7,
        out_specs=(vmem, vmem),
        scratch_shapes=[
            pltpu.VMEM(adjoint_start.shape, f32),
            pltpu.VMEM(vertical_mixing.shape, f32),
            pltpu.VMEM(base_flux.shape, f32),
            pltpu.SMEM(zonal_fraction.shape, f32),
            pltpu.SMEM(meridional_fraction.shape, f32),
            pltpu.SMEM(zonal_hops.shape, jnp.int32),
            pltpu.SMEM(cell_shift.shape, jnp.int32),
            pltpu.SemaphoreType.DMA((7,)),
            pltpu.VMEM((tile, width), jnp.int32),
            pltpu.VMEM((tile, width), jnp.int32),
            pltpu.VMEM((tile, width), f32),
            pltpu.VMEM((tile, width), f32),
            pltpu.VMEM((STEPS, sent, width), f32),
            pltpu.VMEM((STEPS, slots, sent, width), f32),
            pltpu.VMEM((6, tile, width), f32),
            pltpu.VMEM((6, bl, width), f32),
            pltpu.VMEM((tile, width), f32),
            pltpu.VMEM(((rows + 5) * bl, width), f32),
            pltpu.VMEM((tile, width), f32),
            pltpu.VMEM((nbin, rows, width), f32),
            pltpu.SemaphoreType.DMA((STEPS, slots)),
            pltpu.SemaphoreType.DMA((STEPS, slots)),
            pltpu.SemaphoreType.DMA((nbin - 1,)),
            pltpu.SemaphoreType.DMA((nbin - 1,)),
        ],
        compiler_params=pltpu.CompilerParams(
            collective_id=0, has_side_effects=True, vmem_limit_bytes=32 * 1024 * 1024
        ),
    )(
        adjoint_start,
        base_flux,
        vertical_mixing,
        zonal_fraction,
        meridional_fraction,
        zonal_hops,
        cell_shift,
    )


def solution(mesh):
    return jax.shard_map(
        functools.partial(per_device, mesh.shape["lon"], mesh.shape["bin"]),
        mesh=mesh,
        in_specs=(
            P("bin", None, None, "lon"),
            P("bin", None, "lon"),
            P(None, None, "lon"),
            P(),
            P(),
            P(),
            P(),
        ),
        out_specs=(P("bin", None, None, "lon"), P(None, "lon")),
        check_vma=False,
    )
```

```python
import functools

import jax
import jax.numpy as jnp
from jax import lax
from jax.experimental import pallas as pl
from jax.experimental.pallas import tpu as pltpu
from jax.sharding import PartitionSpec as P

HMAX = 3
STEPS = 2
MESH = pl.DeviceIdType.MESH

right_face = (0.0, -1.0, 7.0, 7.0, -1.0)
slope_face = (1.0, -8.0, 0.0, 8.0, -1.0)
curve_face = (3.0, -18.0, 30.0, -18.0, 3.0)


def flux_weights(courant):
    square = courant * courant
    cubic_part = 0.5 * square * (1.0 - courant * (2.0 / 3.0))
    return [
        (
            courant * right_face[offset]
            - 0.5 * square * slope_face[offset]
            + cubic_part * curve_face[offset]
        )
        * (1.0 / 12.0)
        for offset in range(5)
    ]


def taps(courant):
    a = flux_weights(courant)
    return [-a[4], a[4] - a[3], 1.0 + a[3] - a[2], a[2] - a[1], a[1] - a[0], a[0]]


def loop(count, body):
    if count <= 8:
        for i in range(count):
            body(i)
    else:

        @pl.loop(0, count)
        def _(i):
            body(i)


class Plan:
    def __init__(self, rows, unit, ring):
        self.ring = ring
        count = {h: unit for h in range(-HMAX, HMAX + 1)}
        count[0] = rows - 2 * HMAX * unit
        self.count = count
        self.start = {}
        at = 0
        for h in range(-HMAX, HMAX + 1):
            self.start[h] = at
            at += count[h]
        self.rows = rows
        self.extra = 2 * unit
        groups = {}
        for t in range(-HMAX - 2, HMAX + 2):
            if t % ring:
                groups.setdefault(t % ring, []).append(t)
        self.shifts = sorted(groups, key=lambda r: min(r, ring - r))
        self.slot = {r: i for i, r in enumerate(self.shifts)}
        self.part, self.lift = {}, {}
        for r, both in groups.items():
            first, count = self.span(both[0])
            self.lift[both[0]] = 0
            if len(both) == 2:
                self.lift[both[1]] = rows
                count = rows - first + self.span(both[1])[1]
            self.part[r] = first, count

    def span(self, t):
        low, high = max(-t - 2, -HMAX), min(-t + 1, HMAX)
        first = self.start[low]
        return first, self.start[high] + self.count[high] - first


def kernel(
    plan,
    nbin,
    adj_hbm,
    flux_hbm,
    mix_hbm,
    zf_hbm,
    mf_hbm,
    hops_hbm,
    cells_hbm,
    end_ref,
    grad_ref,
    adj_ref,
    mix_ref,
    flux_ref,
    zf_ref,
    mf_ref,
    hops_ref,
    cells_ref,
    load_sem,
    rank,
    shifts_of,
    natural_c,
    mixed,
    sends,
    recvs,
    wz,
    wm,
    zonal,
    padded,
    result,
    gbuf,
    send_sem,
    recv_sem,
    gsend_sem,
    grecv_sem,
):
    bins, levels, rows, width = adj_ref.shape
    bl = bins * levels
    ring = plan.ring
    lon, mybin = lax.axis_index("lon"), lax.axis_index("bin")

    pairs = (
        (mix_hbm, mix_ref),
        (adj_hbm, adj_ref),
        (hops_hbm, hops_ref),
        (zf_hbm, zf_ref),
        (cells_hbm, cells_ref),
        (mf_hbm, mf_ref),
        (flux_hbm, flux_ref),
    )
    loads = [
        pltpu.make_async_copy(source, target, load_sem.at[i])
        for i, (source, target) in enumerate(pairs)
    ]
    for load in loads:
        load.start()

    barrier = pltpu.get_barrier_semaphore()
    shifts = plan.shifts
    for t in shifts:
        pl.semaphore_signal(
            barrier, inc=1, device_id=(lax.rem(lon + ring - t, ring), mybin), device_id_type=MESH
        )
    for o in range(1, nbin):
        pl.semaphore_signal(
            barrier, inc=1, device_id=(lon, lax.rem(mybin + nbin - o, nbin)), device_id_type=MESH
        )

    for load in loads[:3]:
        load.wait()

    inverse, ratios, mix = [], [], [mix_ref[l] for l in range(levels - 1)]
    for l in range(levels):
        pivot = 1.0
        if l < levels - 1:
            pivot = pivot + mix[l]
        if l > 0:
            pivot = pivot + mix[l - 1] + mix[l - 1] * ratios[-1]
        inverse.append(1.0 / pivot)
        if l < levels - 1:
            ratios.append(-mix[l] * inverse[l])

    def at(row):
        if isinstance(row, int):
            return pl.ds(row * bl, bl)
        return pl.ds(pl.multiple_of(row * bl, bl), bl)

    def column(index):
        return pl.ds(index, rows, stride=bl)

    def vertical(field):
        for b in range(bins):
            values = []
            for l in range(levels):
                source = field(b, l)
                if l > 0:
                    source = source + mix[l - 1] * values[-1]
                values.append(source * inverse[l])
            solved = values[levels - 1]
            mixed[column(b * levels + levels - 1), :] = solved
            for l in range(levels - 2, -1, -1):
                solved = values[l] - ratios[l] * solved
                mixed[column(b * levels + l), :] = solved

    level_of = lax.rem(lax.broadcasted_iota(jnp.int32, (bl, width), 0), levels)
    lane = lax.broadcasted_iota(jnp.int32, (bl, width), 1)

    def by_level(value):
        out = jnp.full((bl, width), value(0), jnp.float32)
        for l in range(1, levels):
            out = jnp.where(level_of == l, value(l), out)
        return out

    def splat(value):
        return jnp.full((bl, width), value, jnp.int32)

    def fold(one, start):
        if rows <= 8:
            for i in range(rows):
                start = one(i, start)
            return start
        return lax.fori_loop(0, rows, one, start)

    def find_rank(j):
        mine = splat(hops_ref[j])

        def one(i, total):
            ahead = jnp.where(i < j, 1, 0) if rows > 8 else int(i < j)
            return total + jnp.where(splat(hops_ref[i]) < mine + ahead, 1, 0)

        rank[at(j), :] = fold(one, splat(0))

    def ordered(source, p):
        def one(j, value):
            return jnp.where(rank[at(j), :] == p, source(j), value)

        return fold(one, source(0))

    def copies(step):
        found = []
        for r in plan.shifts:
            first, count = plan.part[r]
            part = pl.ds(first * bl, count * bl)
            i = plan.slot[r]
            found.append(
                pltpu.make_async_remote_copy(
                    src_ref=sends.at[step, part],
                    dst_ref=recvs.at[step, i, part],
                    send_sem=send_sem.at[step, i],
                    recv_sem=recv_sem.at[step, i],
                    device_id=(lax.rem(lon + r, ring), mybin),
                    device_id_type=MESH,
                )
            )
        return found

    def natural(b, l):
        return result[column(b * levels + l), :]

    gradient = None
    for step in range(STEPS):
        vertical(natural if step else (lambda b, l: adj_ref[b, l]))

        def arrange(p):
            sends[step, at(p), :] = ordered(lambda j: mixed[at(j), :], p)

        if step == 0:
            loop(rows, find_rank)
        loop(rows, arrange)
        for p in range(plan.extra):
            sends[step, at(rows + p), :] = sends[step, at(p), :]

        if step == 0:
            pl.semaphore_wait(barrier, len(shifts) + nbin - 1)
        moving = copies(step)
        for copy in moving:
            copy.start()

        if step == 0:
            for load in loads[3:]:
                load.wait()

            def courant(j):
                natural_c[at(j), :] = by_level(lambda l: zf_ref[l, j])

            loop(rows, courant)

            def zonal_weights(p):
                fraction = ordered(lambda j: natural_c[at(j), :], p)
                for s, value in enumerate(taps(fraction)):
                    wz[s, at(p), :] = value
                shifts_of[at(p), :] = ordered(lambda j: splat(cells_ref[j]), p)

            loop(rows, zonal_weights)
            for s, value in enumerate(taps(by_level(lambda l: mf_ref[l]))):
                wm[s] = value
            nothing = jnp.zeros((bl, width), jnp.float32)
            for row in (0, 1, rows + 2, rows + 3, rows + 4):
                padded[at(row), :] = nothing
        else:
            gradient = sum(flux_ref[b] * natural(b, 0) for b in range(bins))

        for copy in moving:
            copy.wait_recv()

        for h in range(-HMAX, HMAX + 1):

            def shift(i):
                p = plan.start[h] + i

                def tile(k):
                    t = -h - k
                    if t % ring == 0:
                        return sends[step, at(p), :]
                    return recvs[step, plan.slot[t % ring], at(p + plan.lift[t]), :]

                cells = shifts_of[at(p), :]
                short = cells < 2
                first = cells - 2 + jnp.where(short, width, 0)
                t0, t1, t2, t3 = tile(-1), tile(0), tile(1), tile(2)
                ra = jnp.where(short, t0, t1)
                rb = jnp.where(short, t1, t2)
                rc = jnp.where(short, t2, t3)
                source = jnp.where(lane < width - first, lane + first, lane + first - width)
                ra = jnp.take_along_axis(ra, source, axis=1, mode="promise_in_bounds")
                rb = jnp.take_along_axis(rb, source, axis=1, mode="promise_in_bounds")
                rc = jnp.take_along_axis(rc, source, axis=1, mode="promise_in_bounds")
                inside = lane < width - first
                w0 = jnp.where(inside, ra, rb)
                w1 = jnp.where(inside, rb, rc)
                out = wz[0, at(p), :] * w0
                for s in range(1, 6):
                    moved = pltpu.roll(jnp.where(lane < s, w1, w0), width - s, 1)
                    out = out + wz[s, at(p), :] * moved
                zonal[at(p), :] = out

            loop(plan.count[h], shift)

        def back(j):
            place = rank[at(j), :]

            def one(p, value):
                return jnp.where(place == p, zonal[at(p), :], value)

            padded[at(j + 2), :] = fold(one, zonal[at(0), :])

        loop(rows, back)

        def meridional(j):
            out = wm[0] * padded[at(j), :]
            for s in range(1, 6):
                out = out + wm[s] * padded[at(j + s), :]
            result[at(j), :] = out

        loop(rows, meridional)

    gradient = gradient + sum(flux_ref[b] * natural(b, 0) for b in range(bins))
    gbuf[mybin] = gradient
    reducing = []
    for o in range(1, nbin):
        copy = pltpu.make_async_remote_copy(
            src_ref=gbuf.at[mybin],
            dst_ref=gbuf.at[mybin],
            send_sem=gsend_sem.at[o - 1],
            recv_sem=grecv_sem.at[o - 1],
            device_id=(lon, lax.rem(mybin + o, nbin)),
            device_id_type=MESH,
        )
        copy.start()
        reducing.append(copy)
    for b in range(bins):
        for l in range(levels):
            end_ref[b, l] = natural(b, l)
    for step in range(STEPS):
        for copy in copies(step):
            copy.wait_send()
    for o in range(1, nbin):
        source = lax.rem(mybin + nbin - o, nbin)
        pltpu.make_async_remote_copy(
            src_ref=gbuf.at[source],
            dst_ref=gbuf.at[source],
            send_sem=gsend_sem.at[o - 1],
            recv_sem=grecv_sem.at[o - 1],
            device_id=(lon, lax.rem(mybin + o, nbin)),
            device_id_type=MESH,
        ).wait_recv()
    total = gbuf[0]
    for o in range(1, nbin):
        total = total + gbuf[o]
    grad_ref[...] = total
    for copy in reducing:
        copy.wait_send()


def per_device(
    ring,
    nbin,
    adjoint_start,
    base_flux,
    vertical_mixing,
    zonal_fraction,
    meridional_fraction,
    zonal_hops,
    cell_shift,
):
    bins, levels, rows, width = adjoint_start.shape
    bl = bins * levels
    plan = Plan(rows, max(1, rows // 16), ring)
    slots = len(plan.shifts)
    sent = (rows + plan.extra) * bl
    vmem = pl.BlockSpec(memory_space=pltpu.VMEM)
    f32 = jnp.float32
    tile = rows * bl
    return pl.pallas_call(
        functools.partial(kernel, plan, nbin),
        out_shape=(
            jax.ShapeDtypeStruct(adjoint_start.shape, f32),
            jax.ShapeDtypeStruct((rows, width), f32),
        ),
        in_specs=[pl.BlockSpec(memory_space=pltpu.HBM)] * 7,
        out_specs=(vmem, vmem),
        scratch_shapes=[
            pltpu.VMEM(adjoint_start.shape, f32),
            pltpu.VMEM(vertical_mixing.shape, f32),
            pltpu.VMEM(base_flux.shape, f32),
            pltpu.SMEM(zonal_fraction.shape, f32),
            pltpu.SMEM(meridional_fraction.shape, f32),
            pltpu.SMEM(zonal_hops.shape, jnp.int32),
            pltpu.SMEM(cell_shift.shape, jnp.int32),
            pltpu.SemaphoreType.DMA((7,)),
            pltpu.VMEM((tile, width), jnp.int32),
            pltpu.VMEM((tile, width), jnp.int32),
            pltpu.VMEM((tile, width), f32),
            pltpu.VMEM((tile, width), f32),
            pltpu.VMEM((STEPS, sent, width), f32),
            pltpu.VMEM((STEPS, slots, sent, width), f32),
            pltpu.VMEM((6, tile, width), f32),
            pltpu.VMEM((6, bl, width), f32),
            pltpu.VMEM((tile, width), f32),
            pltpu.VMEM(((rows + 5) * bl, width), f32),
            pltpu.VMEM((tile, width), f32),
            pltpu.VMEM((nbin, rows, width), f32),
            pltpu.SemaphoreType.DMA((STEPS, slots)),
            pltpu.SemaphoreType.DMA((STEPS, slots)),
            pltpu.SemaphoreType.DMA((nbin - 1,)),
            pltpu.SemaphoreType.DMA((nbin - 1,)),
        ],
        compiler_params=pltpu.CompilerParams(
            collective_id=0, has_side_effects=True, vmem_limit_bytes=32 * 1024 * 1024
        ),
    )(
        adjoint_start,
        base_flux,
        vertical_mixing,
        zonal_fraction,
        meridional_fraction,
        zonal_hops,
        cell_shift,
    )


def solution(mesh):
    return jax.shard_map(
        functools.partial(per_device, mesh.shape["lon"], mesh.shape["bin"]),
        mesh=mesh,
        in_specs=(
            P("bin", None, None, "lon"),
            P("bin", None, "lon"),
            P(None, None, "lon"),
            P(),
            P(),
            P(),
            P(),
        ),
        out_specs=(P("bin", None, None, "lon"), P(None, "lon")),
        check_vma=False,
    )
```

```python
import functools

import jax
import jax.numpy as jnp
from jax import lax
from jax.experimental import pallas as pl
from jax.experimental.pallas import tpu as pltpu
from jax.sharding import PartitionSpec as P

HMAX = 3
STEPS = 2
MESH = pl.DeviceIdType.MESH

right_face = (0.0, -1.0, 7.0, 7.0, -1.0)
slope_face = (1.0, -8.0, 0.0, 8.0, -1.0)
curve_face = (3.0, -18.0, 30.0, -18.0, 3.0)


def flux_weights(courant):
    square = courant * courant
    cubic_part = 0.5 * square * (1.0 - courant * (2.0 / 3.0))
    return [
        (
            courant * right_face[offset]
            - 0.5 * square * slope_face[offset]
            + cubic_part * curve_face[offset]
        )
        * (1.0 / 12.0)
        for offset in range(5)
    ]


def taps(courant):
    a = flux_weights(courant)
    return [-a[4], a[4] - a[3], 1.0 + a[3] - a[2], a[2] - a[1], a[1] - a[0], a[0]]


def loop(count, body):
    if count <= 8:
        for i in range(count):
            body(i)
    else:

        @pl.loop(0, count)
        def _(i):
            body(i)


class Plan:
    def __init__(self, rows, unit, ring):
        self.ring = ring
        count = {h: unit for h in range(-HMAX, HMAX + 1)}
        count[0] = rows - 2 * HMAX * unit
        self.count = count
        self.start = {}
        at = 0
        for h in range(-HMAX, HMAX + 1):
            self.start[h] = at
            at += count[h]
        self.rows = rows
        self.extra = 2 * unit
        groups = {}
        for t in range(-HMAX - 2, HMAX + 2):
            if t % ring:
                groups.setdefault(t % ring, []).append(t)
        self.shifts = sorted(groups, key=lambda r: min(r, ring - r))
        self.slot = {r: i for i, r in enumerate(self.shifts)}
        self.part, self.lift = {}, {}
        for r, both in groups.items():
            first, count = self.span(both[0])
            self.lift[both[0]] = 0
            if len(both) == 2:
                self.lift[both[1]] = rows
                count = rows - first + self.span(both[1])[1]
            self.part[r] = first, count

    def span(self, t):
        low, high = max(-t - 2, -HMAX), min(-t + 1, HMAX)
        first = self.start[low]
        return first, self.start[high] + self.count[high] - first


def kernel(
    plan,
    nbin,
    adj_hbm,
    flux_hbm,
    mix_hbm,
    zf_hbm,
    mf_hbm,
    hops_hbm,
    cells_hbm,
    end_ref,
    grad_ref,
    adj_ref,
    mix_ref,
    flux_ref,
    zf_ref,
    mf_ref,
    hops_ref,
    cells_ref,
    load_sem,
    rank,
    shifts_of,
    natural_c,
    mixed,
    sends,
    recvs,
    wz,
    wm,
    zonal,
    padded,
    result,
    gbuf,
    send_sem,
    recv_sem,
    gsend_sem,
    grecv_sem,
):
    bins, levels, rows, width = adj_ref.shape
    bl = bins * levels
    ring = plan.ring
    lon, mybin = lax.axis_index("lon"), lax.axis_index("bin")

    barrier = pltpu.get_barrier_semaphore()
    shifts = plan.shifts
    for t in shifts:
        pl.semaphore_signal(
            barrier, inc=1, device_id=(lax.rem(lon + ring - t, ring), mybin), device_id_type=MESH
        )
    for o in range(1, nbin):
        pl.semaphore_signal(
            barrier, inc=1, device_id=(lon, lax.rem(mybin + nbin - o, nbin)), device_id_type=MESH
        )

    pairs = (
        (mix_hbm, mix_ref),
        (adj_hbm, adj_ref),
        (hops_hbm, hops_ref),
        (zf_hbm, zf_ref),
        (cells_hbm, cells_ref),
        (mf_hbm, mf_ref),
        (flux_hbm, flux_ref),
    )
    loads = [
        pltpu.make_async_copy(source, target, load_sem.at[i])
        for i, (source, target) in enumerate(pairs)
    ]
    for load in loads:
        load.start()

    for load in loads[:3]:
        load.wait()

    inverse, ratios, mix = [], [], [mix_ref[l] for l in range(levels - 1)]
    for l in range(levels):
        pivot = 1.0
        if l < levels - 1:
            pivot = pivot + mix[l]
        if l > 0:
            pivot = pivot + mix[l - 1] + mix[l - 1] * ratios[-1]
        inverse.append(1.0 / pivot)
        if l < levels - 1:
            ratios.append(-mix[l] * inverse[l])

    def at(row):
        if isinstance(row, int):
            return pl.ds(row * bl, bl)
        return pl.ds(pl.multiple_of(row * bl, bl), bl)

    def column(index):
        return pl.ds(index, rows, stride=bl)

    def vertical(field):
        for b in range(bins):
            values = []
            for l in range(levels):
                source = field(b, l)
                if l > 0:
                    source = source + mix[l - 1] * values[-1]
                values.append(source * inverse[l])
            solved = values[levels - 1]
            mixed[column(b * levels + levels - 1), :] = solved
            for l in range(levels - 2, -1, -1):
                solved = values[l] - ratios[l] * solved
                mixed[column(b * levels + l), :] = solved

    level_of = lax.rem(lax.broadcasted_iota(jnp.int32, (bl, width), 0), levels)
    lane = lax.broadcasted_iota(jnp.int32, (bl, width), 1)

    def by_level(value):
        out = jnp.full((bl, width), value(0), jnp.float32)
        for l in range(1, levels):
            out = jnp.where(level_of == l, value(l), out)
        return out

    def splat(value):
        return jnp.full((bl, width), value, jnp.int32)

    def fold(one, start):
        if rows <= 8:
            for i in range(rows):
                start = one(i, start)
            return start
        return lax.fori_loop(0, rows, one, start)

    def find_rank(j):
        mine = splat(hops_ref[j])

        def one(i, total):
            ahead = jnp.where(i < j, 1, 0) if rows > 8 else int(i < j)
            return total + jnp.where(splat(hops_ref[i]) < mine + ahead, 1, 0)

        rank[at(j), :] = fold(one, splat(0))

    def ordered(source, p):
        def one(j, value):
            return jnp.where(rank[at(j), :] == p, source(j), value)

        return fold(one, source(0))

    def copies(step):
        found = []
        for r in plan.shifts:
            first, count = plan.part[r]
            part = pl.ds(first * bl, count * bl)
            i = plan.slot[r]
            found.append(
                pltpu.make_async_remote_copy(
                    src_ref=sends.at[step, part],
                    dst_ref=recvs.at[step, i, part],
                    send_sem=send_sem.at[step, i],
                    recv_sem=recv_sem.at[step, i],
                    device_id=(lax.rem(lon + r, ring), mybin),
                    device_id_type=MESH,
                )
            )
        return found

    def natural(b, l):
        return result[column(b * levels + l), :]

    gradient = None
    for step in range(STEPS):
        vertical(natural if step else (lambda b, l: adj_ref[b, l]))

        def arrange(p):
            sends[step, at(p), :] = ordered(lambda j: mixed[at(j), :], p)

        if step == 0:
            loop(rows, find_rank)
        loop(rows, arrange)
        for p in range(plan.extra):
            sends[step, at(rows + p), :] = sends[step, at(p), :]

        if step == 0:
            for load in loads[3:]:
                load.wait()

            def courant(j):
                natural_c[at(j), :] = by_level(lambda l: zf_ref[l, j])

            loop(rows, courant)

            def zonal_weights(p):
                fraction = ordered(lambda j: natural_c[at(j), :], p)
                for s, value in enumerate(taps(fraction)):
                    wz[s, at(p), :] = value
                shifts_of[at(p), :] = ordered(lambda j: splat(cells_ref[j]), p)

            loop(rows, zonal_weights)
            for s, value in enumerate(taps(by_level(lambda l: mf_ref[l]))):
                wm[s] = value
            nothing = jnp.zeros((bl, width), jnp.float32)
            for row in (0, 1, rows + 2, rows + 3, rows + 4):
                padded[at(row), :] = nothing
            pl.semaphore_wait(barrier, len(shifts) + nbin - 1)
        moving = copies(step)
        for copy in moving:
            copy.start()

        if step:
            gradient = sum(flux_ref[b] * natural(b, 0) for b in range(bins))

        for copy in moving:
            copy.wait_recv()

        for h in range(-HMAX, HMAX + 1):

            def shift(i):
                p = plan.start[h] + i

                def tile(k):
                    t = -h - k
                    if t % ring == 0:
                        return sends[step, at(p), :]
                    return recvs[step, plan.slot[t % ring], at(p + plan.lift[t]), :]

                cells = shifts_of[at(p), :]
                short = cells < 2
                first = cells - 2 + jnp.where(short, width, 0)
                t0, t1, t2, t3 = tile(-1), tile(0), tile(1), tile(2)
                ra = jnp.where(short, t0, t1)
                rb = jnp.where(short, t1, t2)
                rc = jnp.where(short, t2, t3)
                source = jnp.where(lane < width - first, lane + first, lane + first - width)
                ra = jnp.take_along_axis(ra, source, axis=1, mode="promise_in_bounds")
                rb = jnp.take_along_axis(rb, source, axis=1, mode="promise_in_bounds")
                rc = jnp.take_along_axis(rc, source, axis=1, mode="promise_in_bounds")
                inside = lane < width - first
                w0 = jnp.where(inside, ra, rb)
                w1 = jnp.where(inside, rb, rc)
                out = wz[0, at(p), :] * w0
                for s in range(1, 6):
                    moved = pltpu.roll(jnp.where(lane < s, w1, w0), width - s, 1)
                    out = out + wz[s, at(p), :] * moved
                zonal[at(p), :] = out

            loop(plan.count[h], shift)

        def back(j):
            place = rank[at(j), :]

            def one(p, value):
                return jnp.where(place == p, zonal[at(p), :], value)

            padded[at(j + 2), :] = fold(one, zonal[at(0), :])

        loop(rows, back)

        def meridional(j):
            out = wm[0] * padded[at(j), :]
            for s in range(1, 6):
                out = out + wm[s] * padded[at(j + s), :]
            result[at(j), :] = out

        loop(rows, meridional)

    gradient = gradient + sum(flux_ref[b] * natural(b, 0) for b in range(bins))
    gbuf[mybin] = gradient
    reducing = []
    for o in range(1, nbin):
        copy = pltpu.make_async_remote_copy(
            src_ref=gbuf.at[mybin],
            dst_ref=gbuf.at[mybin],
            send_sem=gsend_sem.at[o - 1],
            recv_sem=grecv_sem.at[o - 1],
            device_id=(lon, lax.rem(mybin + o, nbin)),
            device_id_type=MESH,
        )
        copy.start()
        reducing.append(copy)
    for b in range(bins):
        for l in range(levels):
            end_ref[b, l] = natural(b, l)
    for step in range(STEPS):
        for copy in copies(step):
            copy.wait_send()
    for o in range(1, nbin):
        source = lax.rem(mybin + nbin - o, nbin)
        pltpu.make_async_remote_copy(
            src_ref=gbuf.at[source],
            dst_ref=gbuf.at[source],
            send_sem=gsend_sem.at[o - 1],
            recv_sem=grecv_sem.at[o - 1],
            device_id=(lon, lax.rem(mybin + o, nbin)),
            device_id_type=MESH,
        ).wait_recv()
    total = gbuf[0]
    for o in range(1, nbin):
        total = total + gbuf[o]
    grad_ref[...] = total
    for copy in reducing:
        copy.wait_send()


def per_device(
    ring,
    nbin,
    adjoint_start,
    base_flux,
    vertical_mixing,
    zonal_fraction,
    meridional_fraction,
    zonal_hops,
    cell_shift,
):
    bins, levels, rows, width = adjoint_start.shape
    bl = bins * levels
    plan = Plan(rows, max(1, rows // 16), ring)
    slots = len(plan.shifts)
    sent = (rows + plan.extra) * bl
    vmem = pl.BlockSpec(memory_space=pltpu.VMEM)
    f32 = jnp.float32
    tile = rows * bl
    return pl.pallas_call(
        functools.partial(kernel, plan, nbin),
        out_shape=(
            jax.ShapeDtypeStruct(adjoint_start.shape, f32),
            jax.ShapeDtypeStruct((rows, width), f32),
        ),
        in_specs=[pl.BlockSpec(memory_space=pltpu.HBM)] * 7,
        out_specs=(vmem, vmem),
        scratch_shapes=[
            pltpu.VMEM(adjoint_start.shape, f32),
            pltpu.VMEM(vertical_mixing.shape, f32),
            pltpu.VMEM(base_flux.shape, f32),
            pltpu.SMEM(zonal_fraction.shape, f32),
            pltpu.SMEM(meridional_fraction.shape, f32),
            pltpu.SMEM(zonal_hops.shape, jnp.int32),
            pltpu.SMEM(cell_shift.shape, jnp.int32),
            pltpu.SemaphoreType.DMA((7,)),
            pltpu.VMEM((tile, width), jnp.int32),
            pltpu.VMEM((tile, width), jnp.int32),
            pltpu.VMEM((tile, width), f32),
            pltpu.VMEM((tile, width), f32),
            pltpu.VMEM((STEPS, sent, width), f32),
            pltpu.VMEM((STEPS, slots, sent, width), f32),
            pltpu.VMEM((6, tile, width), f32),
            pltpu.VMEM((6, bl, width), f32),
            pltpu.VMEM((tile, width), f32),
            pltpu.VMEM(((rows + 5) * bl, width), f32),
            pltpu.VMEM((tile, width), f32),
            pltpu.VMEM((nbin, rows, width), f32),
            pltpu.SemaphoreType.DMA((STEPS, slots)),
            pltpu.SemaphoreType.DMA((STEPS, slots)),
            pltpu.SemaphoreType.DMA((nbin - 1,)),
            pltpu.SemaphoreType.DMA((nbin - 1,)),
        ],
        compiler_params=pltpu.CompilerParams(
            collective_id=0, has_side_effects=True, vmem_limit_bytes=32 * 1024 * 1024
        ),
    )(
        adjoint_start,
        base_flux,
        vertical_mixing,
        zonal_fraction,
        meridional_fraction,
        zonal_hops,
        cell_shift,
    )


def solution(mesh):
    return jax.shard_map(
        functools.partial(per_device, mesh.shape["lon"], mesh.shape["bin"]),
        mesh=mesh,
        in_specs=(
            P("bin", None, None, "lon"),
            P("bin", None, "lon"),
            P(None, None, "lon"),
            P(),
            P(),
            P(),
            P(),
        ),
        out_specs=(P("bin", None, None, "lon"), P(None, "lon")),
        check_vma=False,
    )
```
